32 devices in a mesh: parts: 2 (over x), ctx: 8 (over z, y), head: 2 (over core).
Axes of the slice: x: 2, y: 2, z: 4, core: 2. Of those that a mesh axis runs over, the one named last changes fastest.
Arguments:
- channels: bfloat16 [2048, 2048], P(('parts', 'ctx'), 'head'), parts along dimension 0, may hold values from -6 to 6
- gate_channels: bfloat16 [2048, 2048], P(('parts', 'ctx'), 'head'), parts along dimension 0, may hold values from -6 to 6
- bmat: bfloat16 [2048, 512], P(('parts', 'ctx'), 'head'), parts along dimension 0, may hold values from -4 to 4
- cmat: bfloat16 [2048, 512], P(('parts', 'ctx'), 'head'), parts along dimension 0, may hold values from -4 to 4
- dt: float32 [2048, 32], P(('parts', 'ctx'), 'head'), parts along dimension 0, may hold values from 0.1 to 40
- rates: float32 [32], P('head'), may hold values from 0.00029296876 to 0.03
- skip: float32 [32], P('head'), may hold values from 0.5 to 2
- norm_gain: float32 [2048], P('head'), may hold values from 0.25 to 1.75
- docs: int32 [2048], P(('parts', 'ctx')), parts along dimension 0, may hold values from 0 to 3, never falling along the last dimension, each value on 1 to 512 neighbouring positions
- w_out: bfloat16 [2048, 2688], P('head', 'ctx'), may hold values from -0.125 to 0.125
- residual: bfloat16 [2048, 2688], P(('parts', 'ctx', 'head')), parts along dimension 0, may hold values from -6 to 6
- moe_gain: float32 [2688], replicated, may hold values from 0.25 to 1.75
- experts: int32 [2048, 6], P(('parts', 'ctx', 'head')), parts along dimension 0, may hold values from 0 to 15, all different within a row; in each aligned block of 64 rows (0 to 63, 64 to 127, ...) at most 36 rows name the same one
- gates: float32 [2048, 6], P(('parts', 'ctx', 'head')), parts along dimension 0, may hold values from 0.05 to 0.5
- w_up: bfloat16 [16, 2688, 928], P(('ctx', 'head')), may hold values from -0.125 to 0.125
- w_down: bfloat16 [16, 928, 2688], P(('ctx', 'head')), may hold values from -0.1875 to 0.1875
Outputs:
- layer_out: bfloat16 [2048, 2688], P(('parts', 'ctx', 'head')), parts along dimension 0
The draws below stay inside these ranges and needn't reach their ends.
There are 2 independent parts, one for each index of `parts`. The reference program is written for one: setup_inputs(seed, part) draws one part's arguments, and reference() takes and returns one part's arrays. A program takes and returns all parts, laid end to end along the dimension named above; an argument that names none is the same for every part. Nothing has to cross between parts.
Inputs may be any that keep to these rules, and one draw needn't show every extreme that they name: Each row names 6 different experts; in each aligned block of 64 rows (the rows of one device) no expert is named by more than 36 rows. `docs`: ids never fall along the tokens; a document starts where the id changes and holds at most half of the 1024 tokens.
All inputs are finite; a program needn't handle non-finite values.
Results may differ from the reference program's by a relative error of at most 0.013.
Values may be sent and summed in bfloat16 or wider, within the bound.
A program may use at most 128 MiB of HBM per device.

```python
import math
import jax
import jax.numpy as jnp
import numpy as np
from jax import lax

D = 2688
HEADS = 32
HEAD_DIM = 64
GROUPS = 4
STATE = 128
FF = 928
TOP = 6
TOKENS = 1024
ROWS_DEV = 64
EXPERTS = 16
CAP = 36
N_CTX = 8


def draw_dt(key, part):
    key = jax.random.fold_in(key, 11)
    first, second, third = jax.random.split(key, 3)
    level = jax.random.uniform(first, (TOKENS, HEADS), jnp.float32, -0.8, 0.8)
    rough = jnp.exp(level)
    spots = jax.random.randint(second, (8,), 0, TOKENS)
    height = jax.random.uniform(third, (8,), jnp.float32, 10.0, 40.0)
    lifted = jnp.zeros((TOKENS,), jnp.float32).at[spots].max(height)
    return jnp.maximum(rough, lifted[:, None])


def steps_of(stream_key, dims, pieces, smallest, top_value):
    level = 1.0
    for position, blocks in pieces:
        draws = jax.random.uniform(jax.random.fold_in(jax.random.fold_in(stream_key, 6), position), (blocks,), jnp.float32, smallest / len(pieces), top_value / len(pieces))
        level = level * jnp.repeat(jnp.exp(draws), dims[position] // blocks).reshape((-1,) + (1,) * (len(dims) - 1 - position))
    return level


def profile(amount, total, limit, lean):
    portions = [(1 << 20) // math.isqrt(rank ** lean) + 1 for rank in range(2, amount + 1)]
    spare, given = total - limit - (amount - 1), [1] * (amount - 1)
    while spare > 0:
        candidates = [i for i in range(amount - 1) if given[i] < limit]
        whole, budget = sum([portions[i] for i in candidates]), spare
        for i in candidates:
            addition = min(limit - given[i], max(1, budget * portions[i] // whole), spare)
            given[i] = given[i] + addition
            spare = spare - addition
    return np.array([limit] + given)


def uneven_parts(stream_key, amount, total, limit, skew):
    if amount == 2:
        one = jax.random.randint(stream_key, (), max(1, total - limit), min(limit, total - 1) + 1)
        return jnp.stack([one, total - one])
    sizes = jnp.asarray(profile(amount, total, limit, skew), jnp.int32)
    pairs = (amount - 1) // 2
    source_of, sink = sizes[1:1 + 2 * pairs:2], sizes[2:2 + 2 * pairs:2]
    margin = jnp.minimum(source_of - 1, limit - sink)
    shifted = jax.random.randint(jax.random.fold_in(stream_key, 1), (pairs,), 0, 1 << 20) % (margin + 1)
    sizes = sizes.at[1:1 + 2 * pairs:2].set(source_of - shifted).at[2:2 + 2 * pairs:2].set(sink + shifted)
    return sizes[jax.random.permutation(jax.random.fold_in(stream_key, 2), amount)]


def deal_out(rng, own, number, rows, number_of, top, most, lean):
    order = jax.random.permutation(rng, number_of)
    packed, usual = portions_of(number_of, rows * top, most, lean, True), portions_of(number_of, rows * top, most, lean, False)
    places = jnp.arange(number_of)

    def named(lengths, turn):
        used = int((lengths > 0).sum())
        fixed = max(1, used // 4)
        shifted = fixed + (places - fixed + turn * (used - fixed)) % max(1, number_of - fixed)
        return jnp.zeros((number_of,), jnp.int32).at[order[jnp.where(places < fixed, places, shifted)]].set(jnp.asarray(lengths, jnp.int32))

    lengths = jnp.where(number % 4 == 0, named(packed, number // 4), named(usual, number - number // 4 - 1))
    mixed = jax.random.permutation(jax.random.fold_in(own, 3), number_of)
    donor, receiver = mixed[0:number_of // 2 * 2:2], mixed[1:number_of // 2 * 2:2]
    margin = jnp.minimum(lengths[donor] - 1, most - lengths[receiver]) // 2
    margin = jnp.where((donor == order[0]) | (receiver == order[0]) | (lengths[receiver] == 0), 0, jnp.maximum(margin, 0))
    shifted = jax.random.randint(jax.random.fold_in(own, 4), (number_of // 2,), 0, 1 << 20) % (margin + 1)
    lengths = lengths.at[donor].add(-shifted).at[receiver].add(shifted)
    items = jnp.searchsorted(jnp.cumsum(lengths), jnp.arange(rows * top), side="right").astype(jnp.int32)
    listing = items.reshape(top, rows).T
    listing = listing[jax.random.permutation(jax.random.fold_in(own, 1), rows)]
    turn = jax.random.randint(jax.random.fold_in(own, 2), (rows, 1), 0, top)
    return jnp.take_along_axis(listing, (jnp.arange(top)[None, :] + turn) % top, axis=1)


def portions_of(number_of, total, reach, slope, full):
    loads = [(1 << 20) // math.isqrt(grade ** slope) + 1 for grade in range(1, number_of + 1)]
    largest = reach if full else min(reach, max(-(-total // number_of), total * loads[0] // sum(loads)))
    least = 1 if total - largest >= number_of - 1 else 0
    holding, surplus = [largest] + [least] * (number_of - 1), total - largest - least * (number_of - 1)
    while surplus > 0:
        movable = [i for i in range(1, number_of) if holding[i] < largest] or [i for i in range(1, number_of) if holding[i] < reach]
        pool, remaining = sum([loads[i] for i in movable]), surplus
        for i in movable:
            more = min(reach - holding[i], max(1, remaining * loads[i] // pool), surplus)
            holding[i] = holding[i] + more
            surplus = surplus - more
    return np.array(holding)


def gaussian(stream_key, dims, scale, bound, cuts=(), kind=jnp.bfloat16):
    level = steps_of(stream_key, dims, cuts, -0.22, 0.18) if cuts else 1.0
    result = jax.random.normal(stream_key, dims, jnp.float32) * scale * level
    return jnp.minimum(jnp.maximum(result, -bound), bound).astype(kind)


def setup_inputs(seed: int = 0, part: int = 0) -> dict:
    arg_keys = jax.random.split(jax.random.key(seed), 17)
    own_keys = jax.random.split(jax.random.fold_in(arg_keys[16], part), 17)
    channels = gaussian(own_keys[0], (TOKENS, HEADS * HEAD_DIM), 1.0, 6.0, ((0, 8), (1, 2)))
    gate_channels = gaussian(own_keys[1], (TOKENS, HEADS * HEAD_DIM), 1.0, 6.0, ((0, 8), (1, 2)))
    bmat = gaussian(own_keys[2], (TOKENS, GROUPS * STATE), (STATE ** -0.25), 4.0, ((0, 8), (1, 2)))
    cmat = gaussian(own_keys[3], (TOKENS, GROUPS * STATE), (STATE ** -0.25), 4.0, ((0, 8), (1, 2)))
    dt = draw_dt(jax.random.fold_in(jax.random.fold_in(arg_keys[16], part), 71), part)
    rates = jnp.clip(jnp.exp(math.log(0.03) - 4.6288867 * jax.random.uniform(arg_keys[5], (HEADS,), jnp.float32) ** steps_of(arg_keys[5], (HEADS,), ((0, 2),), -0.2, 0.2)), 0.00029296876, 0.03)
    skip = jnp.clip(0.5 + 1.5 * jax.random.uniform(arg_keys[6], (HEADS,), jnp.float32) ** steps_of(arg_keys[6], (HEADS,), ((0, 2),), -0.2, 0.2), 0.5, 2.0)
    norm_gain = jnp.clip(1.0 + 0.15 * jax.random.normal(arg_keys[7], (HEADS * HEAD_DIM,), jnp.float32), 0.25, 1.75)
    docs = jnp.searchsorted(jnp.cumsum(uneven_parts(own_keys[8], max(4, N_CTX // 4), TOKENS, TOKENS // 2, 2)), jnp.arange(TOKENS), side="right").astype(jnp.int32)
    w_out = gaussian(arg_keys[9], (HEADS * HEAD_DIM, D), (HEADS * HEAD_DIM) ** -0.5, 0.125, ((0, 2), (1, 8)))
    residual = gaussian(own_keys[10], (TOKENS, D), 1.0, 6.0, ((0, 16),))
    moe_gain = jnp.clip(1.0 + 0.15 * jax.random.normal(arg_keys[11], (D,), jnp.float32), 0.25, 1.75)
    experts_keys = jax.random.split(jax.random.fold_in(own_keys[12], 1), TOKENS // ROWS_DEV)
    experts_turns = jax.random.permutation(jax.random.fold_in(own_keys[12], 3), TOKENS // ROWS_DEV)
    experts = jax.vmap(lambda own, number: deal_out(jax.random.fold_in(own_keys[12], 2), own, number, ROWS_DEV, EXPERTS, TOP, CAP, 2))(experts_keys, experts_turns).reshape((TOKENS, TOP))
    gates = jnp.clip(jnp.exp(math.log(0.5) - 2.3025851 * jax.random.uniform(own_keys[13], (TOKENS, TOP), jnp.float32) ** steps_of(own_keys[13], (TOKENS, TOP), ((0, 16),), -0.2, 0.2)), 0.05, 0.5)
    w_up = gaussian(arg_keys[14], (EXPERTS, D, FF), D ** -0.5, 0.125, ((0, 16),))
    w_down = gaussian(arg_keys[15], (EXPERTS, FF, D), FF ** -0.5, 0.1875, ((0, 16),))
    return dict(channels=channels, gate_channels=gate_channels, bmat=bmat, cmat=cmat, dt=dt, rates=rates, skip=skip, norm_gain=norm_gain, docs=docs, w_out=w_out, residual=residual, moe_gain=moe_gain, experts=experts, gates=gates, w_up=w_up, w_down=w_down)


EPS = 1e-05
BLOCK_ROWS = 128

def silu(value):
    return value / (1.0 + jnp.exp(-value))

def mamba_scan(channels, bmat, cmat, dt, rates, skip, docs):
    heads = rates.shape[0]
    per_group = heads // GROUPS
    xs = channels.astype(jnp.float32).reshape(TOKENS, heads, HEAD_DIM)
    bs = bmat.astype(jnp.float32).reshape(TOKENS, GROUPS, STATE)
    cs = cmat.astype(jnp.float32).reshape(TOKENS, GROUPS, STATE)
    before = jnp.concatenate([docs[:1] - 1, docs[:-1]])
    keep = (docs == before).astype(jnp.float32)

    def step(state, inputs):
        x_now, b_now, c_now, dt_now, keep_now = inputs
        decay = jnp.exp(-rates * dt_now) * keep_now
        b_heads = jnp.repeat(b_now, per_group, axis=0)
        c_heads = jnp.repeat(c_now, per_group, axis=0)
        state = decay[:, None, None] * state + (dt_now[:, None] * x_now)[:, :, None] * b_heads[:, None, :]
        y_now = lax.optimization_barrier(jnp.sum(state * c_heads[:, None, :], axis=2)) + skip[:, None] * x_now
        return (state, y_now)
    start = jnp.zeros((heads, HEAD_DIM, STATE), jnp.float32)
    _, ys = lax.scan(step, start, (xs, bs, cs, dt, keep))
    return ys.reshape(TOKENS, heads * HEAD_DIM)

def gated_norm(scan, gate_channels, gain):
    gated = scan * silu(gate_channels.astype(jnp.float32))
    width = HEADS * HEAD_DIM // GROUPS
    grouped = gated.reshape(gated.shape[0], -1, width)
    square = lax.optimization_barrier(jnp.mean(grouped * grouped, axis=2, keepdims=True))
    normed = grouped / jnp.sqrt(square + EPS)
    return normed.reshape(gated.shape[0], -1) * gain

def experts_apply(moe_in, experts, gates, w_up, w_down):
    picks = TOKENS * TOP
    flat = experts.reshape(-1).astype(jnp.int32)
    order = jnp.argsort(flat, stable=True).astype(jnp.int32)
    labels = jnp.arange(EXPERTS, dtype=jnp.int32)
    counts = lax.optimization_barrier(jnp.sum((flat[None, :] == labels[:, None]).astype(jnp.int32), axis=1)).astype(jnp.int32)
    starts = (jnp.cumsum(counts) - counts).astype(jnp.int32)
    blocks = ((counts + BLOCK_ROWS - 1) // BLOCK_ROWS).astype(jnp.int32)
    block_ends = jnp.cumsum(blocks).astype(jnp.int32)
    block_starts = (block_ends - blocks).astype(jnp.int32)
    nblocks = picks // BLOCK_ROWS + EXPERTS
    sorted_experts = flat[order]
    rank = jnp.arange(picks, dtype=jnp.int32) - starts[sorted_experts]
    padded = (block_starts[sorted_experts] * BLOCK_ROWS + rank).astype(jnp.int32)
    source_row = jnp.full((nblocks * BLOCK_ROWS,), TOKENS, jnp.int32).at[padded].set(order // TOP)
    block_ids = jnp.arange(nblocks, dtype=jnp.int32)
    owner = lax.optimization_barrier(jnp.sum((block_ends[None, :] <= block_ids[:, None]).astype(jnp.int32), axis=1))
    owner = jnp.minimum(owner, EXPERTS - 1).astype(jnp.int32)
    table = jnp.concatenate([moe_in, jnp.zeros((1, D), jnp.bfloat16)], axis=0)

    def one_block(inputs):
        rows_index, expert = inputs
        rows = table[rows_index].astype(jnp.float32)
        up = jnp.dot(rows, w_up[expert].astype(jnp.float32), preferred_element_type=jnp.float32)
        act = jnp.square(jnp.maximum(up, 0.0)).astype(jnp.bfloat16)
        down = jnp.dot(act.astype(jnp.float32), w_down[expert].astype(jnp.float32), preferred_element_type=jnp.float32)
        return down.astype(jnp.bfloat16)
    results = lax.map(one_block, (source_row.reshape(nblocks, BLOCK_ROWS), owner)).reshape(-1, D)
    pick_pos = jnp.zeros((picks,), jnp.int32).at[order].set(padded)
    chosen = results[pick_pos].reshape(TOKENS, TOP, D).astype(jnp.float32)
    return lax.optimization_barrier(jnp.sum(chosen * gates[:, :, None], axis=1))

def reference(channels, gate_channels, bmat, cmat, dt, rates, skip, norm_gain, docs, w_out, residual, moe_gain, experts, gates, w_up, w_down):
    scan = mamba_scan(channels, bmat, cmat, dt, rates, skip, docs)
    normed_scan = gated_norm(scan, gate_channels, norm_gain).astype(jnp.bfloat16)
    mamba_out = jnp.dot(normed_scan, w_out, preferred_element_type=jnp.float32)
    hidden = (residual.astype(jnp.float32) + mamba_out).astype(jnp.bfloat16)
    widened = hidden.astype(jnp.float32)
    moe_in = (widened / jnp.sqrt(lax.optimization_barrier(jnp.mean(widened * widened, axis=1, keepdims=True)) + EPS) * moe_gain).astype(jnp.bfloat16)
    mixture = experts_apply(moe_in, experts, gates, w_up, w_down)
    return (widened + mixture).astype(jnp.bfloat16)
```

```python
import functools

import jax
import jax.numpy as jnp
from jax import lax
from jax.experimental import pallas as pl
from jax.experimental.pallas import tpu as pltpu
from jax.sharding import PartitionSpec as P

HEADS = 32
HEAD_DIM = 64
GROUPS = 4
STATE = 128


EPS = 1e-05


def entering(array, axis, combine, identity):
    size, place = (lax.axis_size(axis), lax.axis_index(axis))
    everything = jax.tree.map(lambda part: lax.all_gather(part, axis), array)
    start = jax.tree.map(
        lambda part, zero: jnp.broadcast_to(jnp.asarray(zero, part.dtype), part.shape),
        array,
        identity,
    )

    def lap(k, before):
        reached = k < place
        new = combine(before, jax.tree.map(lambda part: part[k], everything))
        return jax.tree.map(lambda a, b: jnp.where(reached, a, b), new, before)

    return lax.fori_loop(0, size, lap, start)


def silu(value):
    return value / (1.0 + jnp.exp(-value))


def combine_states(earlier, later):
    first_a, last_a, decay_a, state_a = earlier
    first_b, last_b, decay_b, state_b = later
    linked = ((last_a == first_b) | (last_a < 0) | (first_b < 0)).astype(jnp.float32)
    carried = decay_b * linked
    decay = carried * decay_a
    state = state_b + carried[:, None, None] * state_a
    first = jnp.where(first_a < 0, first_b, first_a)
    last = jnp.where(last_b < 0, last_a, last_b)
    return (first, last, decay, state)


def group_terms(inputs, causal, ending):
    x_group, b_group, c_group, log_group, dt_group = inputs
    scores = jnp.dot(c_group, b_group.T, preferred_element_type=jnp.float32)
    gap = jnp.where(causal[:, :, None], log_group[:, None, :] - log_group[None, :, :], -jnp.inf)
    weight = jnp.exp(gap) * scores[:, :, None] * dt_group[None, :, :]
    inner = jnp.einsum("tsh,shp->thp", weight, x_group, precision=lax.Precision.HIGHEST)
    tail = jnp.exp(log_group[-1][None, :] - log_group) * ending[:, None] * dt_group
    end_state = jnp.einsum(
        "sh,shp,sn->hpn",
        tail,
        x_group,
        b_group.astype(jnp.float32),
        precision=lax.Precision.HIGHEST,
    )
    return (inner, end_state)


def expert_rows(received, up_weight, down_weight):
    sources, items, width = received.shape
    rows = received.reshape(sources * items, width)
    up = jnp.dot(rows, up_weight, preferred_element_type=jnp.float32)
    act = jnp.square(jnp.maximum(up, 0.0)).astype(jnp.bfloat16)
    result = jnp.dot(act, down_weight, preferred_element_type=jnp.float32).astype(jnp.bfloat16)
    return result.reshape(sources, items, width)


MESH = pl.DeviceIdType.MESH
LANES = 128


def ring_place(index, size):
    half, odd = index // 2, index % 2
    return (1 - odd) * half + odd * (size - 1 - half)


def ring_index(place, size):
    back = place // (size // 2)
    return (1 - back) * (2 * place) + back * (2 * (size - 1 - place) + 1)


def moe_kernel(
    n,
    heads,
    hidden_ref,
    gain_ref,
    gate_ref,
    up_hbm,
    down_hbm,
    out_ref,
    rows_ref,
    part_ref,
    lent_ref,
    borrowed_ref,
    sums_ref,
    act_ref,
    up_ref,
    down_ref,
    weight_sem,
    ag_send,
    ag_recv,
    sib_send,
    sib_recv,
    lend_send,
    lend_recv,
    rs_send,
    rs_recv,
):
    rows, width = hidden_ref.shape
    both = 2 * rows
    inner = up_ref.shape[1]
    half = n // 2
    cut = rows // 2
    place = ring_place(lax.axis_index("ctx"), n)
    head = lax.axis_index("head")
    mine = lax.axis_index("ctx") * heads + head
    after = {"ctx": ring_index((place + 1) % n, n)}
    before = {"ctx": ring_index((place + n - 1) % n, n)}
    sibling = {"head": 1 - head}

    up_copy = pltpu.make_async_copy(up_hbm.at[0], up_ref, weight_sem.at[0])
    down_copy = pltpu.make_async_copy(down_hbm.at[0], down_ref, weight_sem.at[1])
    up_copy.start()
    down_copy.start()

    barrier = pltpu.get_barrier_semaphore()
    for device in (after, before, sibling):
        pl.semaphore_signal(barrier, inc=1, device_id=device, device_id_type=MESH)

    def slot(s):
        if s == 0:
            return 0
        if s == half:
            return 1
        return 2 * s if s < half else 2 * (n - s) + 1

    def send(source, target, send_sem, recv_sem, device):
        copy = pltpu.make_async_remote_copy(
            src_ref=source,
            dst_ref=target,
            send_sem=send_sem,
            recv_sem=recv_sem,
            device_id=device,
            device_id_type=MESH,
        )
        copy.start()
        return copy

    hidden = hidden_ref[...].astype(jnp.float32)
    scale = jnp.sqrt(jnp.mean(hidden * hidden, axis=1, keepdims=True) + EPS)
    rows_ref[pl.ds(0, rows), pl.ds(0, width)] = (hidden / scale * gain_ref[...]).astype(jnp.bfloat16)
    gate = gate_ref[...]
    high = gate.astype(jnp.bfloat16).astype(jnp.float32)
    lane = lax.broadcasted_iota(jnp.int32, gate.shape, 1)
    rows_ref[pl.ds(0, rows), pl.ds(width, LANES)] = jnp.where(lane < LANES // 2, high, gate - high).astype(jnp.bfloat16)

    pl.semaphore_wait(barrier, 3)

    def hop(k):
        lo, size_up, size_down = 0, rows, rows
        start_up, start_down = 0, 0
        if k == half:
            size_up, size_down, start_down = cut, rows - cut, cut
        source_up = rows_ref.at[pl.ds(slot(k - 1) * both + start_up, size_up)]
        target_up = rows_ref.at[pl.ds(slot(k) * both + start_up, size_up)]
        source_down = rows_ref.at[pl.ds(slot((n - k + 1) % n) * both + start_down, size_down)]
        target_down = rows_ref.at[pl.ds(slot(n - k) * both + start_down, size_down)]
        return (
            send(source_up, target_up, ag_send.at[0, k - 1], ag_recv.at[0, k - 1], after),
            send(source_down, target_down, ag_send.at[1, k - 1], ag_recv.at[1, k - 1], before),
        )

    def share(s):
        return send(
            rows_ref.at[pl.ds(slot(s) * both, rows)],
            rows_ref.at[pl.ds(slot(s) * both + rows, rows)],
            sib_send.at[slot(s)],
            sib_recv.at[slot(s)],
            sibling,
        )

    column = lax.broadcasted_iota(jnp.int32, (both, LANES), 1)

    def expert(slots):
        count = len(slots) * both
        first = slots[0]
        block = pl.ds(first * both, count)

        def up(columns):
            value = jnp.dot(
                rows_ref[block, pl.ds(0, width)], up_ref[:, columns], preferred_element_type=jnp.float32
            )
            value = jnp.maximum(value, 0.0)
            act_ref[pl.ds(0, count), columns] = (value * value).astype(jnp.bfloat16)

        tile = 2 * LANES

        @pl.loop(0, inner // tile)
        def _(i):
            up(pl.ds(pl.multiple_of(i * tile, tile), tile))

        if inner % tile:
            up(pl.ds(inner // tile * tile, inner % tile))

        weights = []
        for s in slots:
            carried = rows_ref[pl.ds(s * both, both), pl.ds(width, LANES)].astype(jnp.float32)
            chosen = (column == mine) | (column == mine + LANES // 2)
            weights.append(jnp.sum(jnp.where(chosen, carried, 0.0), axis=1, keepdims=True))

        def down(columns):
            value = jnp.dot(
                act_ref[pl.ds(0, count), :], down_ref[:, columns], preferred_element_type=jnp.float32
            )
            for i, s in enumerate(slots):
                own = value[i * both : i * both + rows] * weights[i][:rows]
                other = value[i * both + rows : (i + 1) * both] * weights[i][rows:]
                part_ref[s, :, columns] = own.astype(jnp.bfloat16)
                lent_ref[s, :, columns] = other.astype(jnp.bfloat16)

        wide = width // LANES
        step = max(d for d in (1, 2, 3, 4) if wide % d == 0) * LANES

        @pl.loop(0, width // step)
        def _(i):
            down(pl.ds(pl.multiple_of(i * step, LANES), step))

        return [
            send(lent_ref.at[s], borrowed_ref.at[s], lend_send.at[s], lend_recv.at[s], sibling) for s in slots
        ]

    loans = {}
    started = list(hop(1))
    arriving = started
    shares = {0: share(0)}
    up_copy.wait()
    down_copy.wait()
    shares[0].wait_recv()
    loans[slot(0)] = expert([slot(0)])[0]
    for k in range(1, half + 1):
        for copy in arriving:
            copy.wait_recv()
        if k < half:
            arriving = hop(k + 1)
            started += list(arriving)
        near = [k, n - k] if k < half else [k]
        for s in near:
            shares[s] = share(s)
        for s in near:
            shares[s].wait_recv()
        lent = expert([slot(s) for s in near])
        for s, copy in zip(near, lent):
            loans[slot(s)] = copy

    def total(s, inbound):
        loans[slot(s)].wait_recv()
        value = part_ref[slot(s)].astype(jnp.float32) + borrowed_ref[slot(s)].astype(jnp.float32)
        return value

    backs = []

    def give(s, low, high, down, k):
        piece = pl.ds(low, high - low)
        if down:
            nearer = s - 1 if s > 1 else 0
            return send(
                part_ref.at[slot(s), piece],
                sums_ref.at[slot(nearer), piece],
                rs_send.at[0, k - 1],
                rs_recv.at[0, k - 1],
                before,
            )
        nearer = s + 1 if s + 1 < n else half
        return send(
            part_ref.at[slot(s), piece],
            sums_ref.at[slot(nearer), piece],
            rs_send.at[1, k - 1],
            rs_recv.at[1, k - 1],
            after,
        )

    part_ref[slot(half)] = total(half, None).astype(jnp.bfloat16)
    coming = [give(half, 0, cut, True, half), give(half, cut, rows, False, half)]
    backs += coming
    for k in range(half - 1, 0, -1):
        lower = total(k, None)
        upper = total(n - k, None)
        part_ref[slot(k)] = lower.astype(jnp.bfloat16)
        part_ref[slot(n - k)] = upper.astype(jnp.bfloat16)
        following = []
        for way, (s, copy) in enumerate(zip((k, n - k), coming)):
            copy.wait_recv()
            piece = pl.ds(0, rows)
            if k == half - 1:
                piece = pl.ds(0, cut) if way == 0 else pl.ds(cut, rows - cut)
            value = part_ref[slot(s), piece].astype(jnp.float32) + sums_ref[slot(s), piece].astype(jnp.float32)
            part_ref[slot(s), piece] = value.astype(jnp.bfloat16)
            following.append(give(s, 0, rows, way == 0, k))
        coming = following
        backs += coming
    value = hidden_ref[...].astype(jnp.float32) + total(0, None)
    for copy in coming:
        copy.wait_recv()
    value = value + sums_ref[slot(0)].astype(jnp.float32) + sums_ref[slot(half)].astype(jnp.float32)
    out_ref[...] = value.astype(jnp.bfloat16)
    for copy in started + list(shares.values()) + list(loans.values()) + backs:
        copy.wait_send()


def moe_on_ring(hidden, moe_gain, experts, gates, w_up, w_down):
    n, heads = lax.axis_size("ctx"), lax.axis_size("head")
    rows, width = hidden.shape
    inner = w_up.shape[2]
    lane = jnp.arange(LANES, dtype=jnp.int32) % (LANES // 2)
    gate = jnp.sum(jnp.where(experts[:, :, None] == lane[None, None, :], gates[:, :, None], 0.0), axis=1)
    vmem = pl.BlockSpec(memory_space=pltpu.VMEM)
    anywhere = pl.BlockSpec(memory_space=pl.ANY)
    pieces = pltpu.VMEM((n, rows, width), jnp.bfloat16)
    return pl.pallas_call(
        functools.partial(moe_kernel, n, heads),
        out_shape=jax.ShapeDtypeStruct((rows, width), jnp.bfloat16),
        in_specs=[vmem, vmem, vmem, anywhere, anywhere],
        out_specs=vmem,
        scratch_shapes=[
            pltpu.VMEM((n * 2 * rows, width + LANES), jnp.bfloat16),
            pieces,
            pieces,
            pieces,
            pieces,
            pltpu.VMEM((4 * rows, inner), jnp.bfloat16),
            pltpu.VMEM((width, inner), jnp.bfloat16),
            pltpu.VMEM((inner, width), jnp.bfloat16),
            pltpu.SemaphoreType.DMA((2,)),
            pltpu.SemaphoreType.DMA((2, n // 2)),
            pltpu.SemaphoreType.DMA((2, n // 2)),
            pltpu.SemaphoreType.DMA((n,)),
            pltpu.SemaphoreType.DMA((n,)),
            pltpu.SemaphoreType.DMA((n,)),
            pltpu.SemaphoreType.DMA((n,)),
            pltpu.SemaphoreType.DMA((2, n // 2)),
            pltpu.SemaphoreType.DMA((2, n // 2)),
        ],
        compiler_params=pltpu.CompilerParams(
            collective_id=1, has_side_effects=True, vmem_limit_bytes=56 * 2**20
        ),
        cost_estimate=pl.CostEstimate(
            flops=8 * n * rows * width * inner, bytes_accessed=4 * width * inner, transcendentals=0
        ),
    )(hidden, moe_gain.reshape(1, width), gate, w_up, w_down)


def ring_fits(n, heads, rows, width):
    return n % 2 == 0 and n >= 4 and heads == 2 and rows % 32 == 0 and width % LANES == 0 and n * heads <= LANES // 2 and 14 * n * rows * width <= 24 * 2**20


def local(
    channels,
    gate_channels,
    bmat,
    cmat,
    dt,
    rates,
    skip,
    norm_gain,
    docs,
    w_out,
    residual,
    moe_gain,
    experts,
    gates,
    w_up,
    w_down,
):
    length = channels.shape[0]
    heads = dt.shape[1]
    groups = bmat.shape[1] // STATE
    per_group = heads // groups
    logs = jnp.cumsum(-rates[None, :] * dt, axis=0)
    x_wide = channels.astype(jnp.float32).reshape(length, groups, per_group, HEAD_DIM)
    b_split = bmat.reshape(length, groups, STATE)
    c_split = cmat.reshape(length, groups, STATE)
    position = jnp.arange(length, dtype=jnp.int32)
    causal = (docs[:, None] == docs[None, :]) & (position[:, None] >= position[None, :])
    ending = (docs == docs[length - 1]).astype(jnp.float32)
    opening = (docs == docs[0]).astype(jnp.float32)
    stacked = (
        x_wide.transpose(1, 0, 2, 3),
        b_split.transpose(1, 0, 2),
        c_split.transpose(1, 0, 2),
        logs.reshape(length, groups, per_group).transpose(1, 0, 2),
        dt.reshape(length, groups, per_group).transpose(1, 0, 2),
    )
    inner, end_state = lax.map(lambda item: group_terms(item, causal, ending), stacked)
    end_state = end_state.reshape(heads, HEAD_DIM, STATE)
    whole_decay = jnp.exp(logs[length - 1]) * (docs[0] == docs[length - 1]).astype(jnp.float32)
    element = (docs[:1], docs[length - 1 :], whole_decay, end_state)
    identity = (
        jnp.full((1,), -1, jnp.int32),
        jnp.full((1,), -1, jnp.int32),
        jnp.ones((heads,), jnp.float32),
        jnp.zeros_like(end_state),
    )
    _, prior_last, _, incoming = entering(element, "ctx", combine_states, identity)
    linked = (prior_last == docs[:1]).astype(jnp.float32)
    reach = jnp.exp(logs) * opening[:, None] * linked
    outer = jnp.einsum(
        "tgn,ghpn->tghp",
        c_split.astype(jnp.float32),
        incoming.reshape(groups, per_group, HEAD_DIM, STATE),
        precision=lax.Precision.HIGHEST,
    )
    outer = outer * reach.reshape(length, groups, per_group)[:, :, :, None]
    inner = inner.transpose(1, 0, 2, 3)
    scan = (inner + outer).reshape(length, heads, HEAD_DIM) + skip[None, :, None] * x_wide.reshape(
        length, heads, HEAD_DIM
    )
    scan = scan.reshape(length, heads * HEAD_DIM)
    gated = scan * silu(gate_channels.astype(jnp.float32))
    grouped = gated.reshape(length, -1, HEADS * HEAD_DIM // GROUPS)
    grouped = grouped / jnp.sqrt(jnp.mean(grouped * grouped, axis=2, keepdims=True) + EPS)
    normed_scan = (grouped.reshape(length, -1) * norm_gain).astype(jnp.bfloat16)
    partial_value = jnp.dot(
        normed_scan,
        lax.all_gather(w_out, "ctx", axis=1, tiled=True),
        preferred_element_type=jnp.float32,
    )
    mamba_out = lax.psum_scatter(
        partial_value.astype(jnp.bfloat16), "head", scatter_dimension=0, tiled=True
    ).astype(jnp.float32)
    hidden = (residual.astype(jnp.float32) + mamba_out).astype(jnp.bfloat16)
    if ring_fits(lax.axis_size("ctx"), lax.axis_size("head"), *hidden.shape):
        return moe_on_ring(hidden, moe_gain, experts, gates, w_up, w_down)
    widened = hidden.astype(jnp.float32)
    moe_in = (
        widened / jnp.sqrt(jnp.mean(widened * widened, axis=1, keepdims=True) + EPS) * moe_gain
    ).astype(jnp.bfloat16)
    rows_dev = moe_in.shape[0]
    top = experts.shape[1]
    width = moe_in.shape[1]
    ctx_count = lax.axis_size("ctx")
    head_count = lax.axis_size("head")
    experts_all = ctx_count * head_count
    capacity = min(rows_dev, max(4, 3 * rows_dev * top // (2 * experts_all)))
    picks = experts.reshape(-1)
    pick_index = jnp.arange(picks.shape[0], dtype=jnp.int32)
    earlier = (picks[:, None] == picks[None, :]) & (pick_index[None, :] < pick_index[:, None])
    slot = jnp.sum(earlier.astype(jnp.int32), axis=1)
    target = (picks * capacity + slot).reshape(rows_dev, top)
    places = jnp.arange(experts_all * capacity, dtype=jnp.int32)
    routing = jnp.any(target[None, :, :] == places[:, None, None], axis=2).astype(jnp.bfloat16)
    outgoing = jnp.dot(routing, moe_in, preferred_element_type=jnp.float32).astype(jnp.bfloat16)
    outgoing = outgoing.reshape(experts_all, capacity, width)
    up_weight = w_up[0]
    down_weight = w_down[0]
    results = expert_rows(
        lax.all_to_all(outgoing, ("ctx", "head"), split_axis=0, concat_axis=0, tiled=True),
        up_weight,
        down_weight,
    )
    returned = lax.all_to_all(results, ("ctx", "head"), split_axis=0, concat_axis=0, tiled=True)
    flat_back = returned.reshape(experts_all * capacity, width)
    chosen = flat_back[target].astype(jnp.float32)
    mixture = jnp.sum(chosen * gates[:, :, None], axis=1)
    return (widened + mixture).astype(jnp.bfloat16)


def solution(mesh):
    return jax.shard_map(
        local,
        mesh=mesh,
        in_specs=(
            P(("parts", "ctx"), "head"),
            P(("parts", "ctx"), "head"),
            P(("parts", "ctx"), "head"),
            P(("parts", "ctx"), "head"),
            P(("parts", "ctx"), "head"),
            P("head"),
            P("head"),
            P("head"),
            P(("parts", "ctx")),
            P("head", "ctx"),
            P(("parts", "ctx", "head"), None),
            P(),
            P(("parts", "ctx", "head"), None),
            P(("parts", "ctx", "head"), None),
            P(("ctx", "head"), None, None),
            P(("ctx", "head"), None, None),
        ),
        out_specs=P(("parts", "ctx", "head"), None),
        check_vma=False,
    )
```

```python
import functools

import jax
import jax.numpy as jnp
from jax import lax
from jax.experimental import pallas as pl
from jax.experimental.pallas import tpu as pltpu
from jax.sharding import PartitionSpec as P

HEADS = 32
HEAD_DIM = 64
GROUPS = 4
STATE = 128


EPS = 1e-05


def entering(array, axis, combine, identity):
    size, place = (lax.axis_size(axis), lax.axis_index(axis))
    everything = jax.tree.map(lambda part: lax.all_gather(part, axis), array)
    start = jax.tree.map(
        lambda part, zero: jnp.broadcast_to(jnp.asarray(zero, part.dtype), part.shape),
        array,
        identity,
    )

    def lap(k, before):
        reached = k < place
        new = combine(before, jax.tree.map(lambda part: part[k], everything))
        return jax.tree.map(lambda a, b: jnp.where(reached, a, b), new, before)

    return lax.fori_loop(0, size, lap, start)


def silu(value):
    return value / (1.0 + jnp.exp(-value))


def combine_states(earlier, later):
    first_a, last_a, decay_a, state_a = earlier
    first_b, last_b, decay_b, state_b = later
    linked = ((last_a == first_b) | (last_a < 0) | (first_b < 0)).astype(jnp.float32)
    carried = decay_b * linked
    decay = carried * decay_a
    state = state_b + carried[:, None, None] * state_a
    first = jnp.where(first_a < 0, first_b, first_a)
    last = jnp.where(last_b < 0, last_a, last_b)
    return (first, last, decay, state)


def group_terms(inputs, causal, ending):
    x_group, b_group, c_group, log_group, dt_group = inputs
    scores = jnp.dot(c_group, b_group.T, preferred_element_type=jnp.float32)
    gap = jnp.where(causal[:, :, None], log_group[:, None, :] - log_group[None, :, :], -jnp.inf)
    weight = jnp.exp(gap) * scores[:, :, None] * dt_group[None, :, :]
    inner = jnp.einsum("tsh,shp->thp", weight, x_group, precision=lax.Precision.HIGHEST)
    tail = jnp.exp(log_group[-1][None, :] - log_group) * ending[:, None] * dt_group
    end_state = jnp.einsum(
        "sh,shp,sn->hpn",
        tail,
        x_group,
        b_group.astype(jnp.float32),
        precision=lax.Precision.HIGHEST,
    )
    return (inner, end_state)


def expert_rows(received, up_weight, down_weight):
    sources, items, width = received.shape
    rows = received.reshape(sources * items, width)
    up = jnp.dot(rows, up_weight, preferred_element_type=jnp.float32)
    act = jnp.square(jnp.maximum(up, 0.0)).astype(jnp.bfloat16)
    result = jnp.dot(act, down_weight, preferred_element_type=jnp.float32).astype(jnp.bfloat16)
    return result.reshape(sources, items, width)


MESH = pl.DeviceIdType.MESH
LANES = 128


def ring_place(index, size):
    half, odd = index // 2, index % 2
    return (1 - odd) * half + odd * (size - 1 - half)


def ring_index(place, size):
    back = place // (size // 2)
    return (1 - back) * (2 * place) + back * (2 * (size - 1 - place) + 1)


def layer_kernel(
    n,
    heads,
    x_ref,
    silu_ref,
    b_ref,
    c_ref,
    dt_ref,
    rates_ref,
    skip_ref,
    norm_ref,
    docs_col_ref,
    docs_row_ref,
    proj_ref,
    residual_ref,
    gain_ref,
    gate_ref,
    up_hbm,
    down_hbm,
    out_ref,
    meta_ref,
    reach_ref,
    state_ref,
    scan_ref,
    incoming_ref,
    normed_ref,
    product_ref,
    product_lent_ref,
    product_got_ref,
    block_ref,
    columns_ref,
    mamba_ref,
    hidden_ref,
    rows_ref,
    part_ref,
    lent_ref,
    borrowed_ref,
    sums_ref,
    act_ref,
    up_ref,
    down_ref,
    weight_sem,
    meta_send,
    meta_recv,
    state_send,
    state_recv,
    normed_send,
    normed_recv,
    product_send,
    product_recv,
    block_send,
    block_recv,
    ag_send,
    ag_recv,
    sib_send,
    sib_recv,
    lend_send,
    lend_recv,
    rs_send,
    rs_recv,
):
    rows, width = residual_ref.shape
    both = 2 * rows
    inner = up_ref.shape[0]
    half = n // 2
    cut = rows // 2
    place = ring_place(lax.axis_index("ctx"), n)
    head = lax.axis_index("head")
    mine = lax.axis_index("ctx") * heads + head
    after = {"ctx": ring_index((place + 1) % n, n)}
    before = {"ctx": ring_index((place + n - 1) % n, n)}
    sibling = {"head": 1 - head}

    up_copy = pltpu.make_async_copy(up_hbm.at[0], up_ref, weight_sem.at[0])
    down_copy = pltpu.make_async_copy(down_hbm.at[0], down_ref, weight_sem.at[1])
    up_copy.start()
    down_copy.start()

    me = lax.axis_index("ctx")
    barrier = pltpu.get_barrier_semaphore()
    for d in range(1, n):
        pl.semaphore_signal(barrier, inc=1, device_id={"ctx": (me + d) % n}, device_id_type=MESH)
    pl.semaphore_signal(barrier, inc=1, device_id=sibling, device_id_type=MESH)

    def slot(s):
        if s == 0:
            return 0
        if s == half:
            return 1
        return 2 * s if s < half else 2 * (n - s) + 1

    def send(source, target, send_sem, recv_sem, device):
        copy = pltpu.make_async_remote_copy(
            src_ref=source,
            dst_ref=target,
            send_sem=send_sem,
            recv_sem=recv_sem,
            device_id=device,
            device_id_type=MESH,
        )
        copy.start()
        return copy

    def ring_hop(ref, stride, size, send_sem, recv_sem, k):
        up_start, up_size, down_start, down_size = 0, size, 0, size
        if k == half:
            up_size, down_start, down_size = size // 2, size // 2, size // 2
        up_from = ref.at[pl.ds(slot(k - 1) * stride + up_start, up_size)]
        up_to = ref.at[pl.ds(slot(k) * stride + up_start, up_size)]
        down_from = ref.at[pl.ds(slot((n - k + 1) % n) * stride + down_start, down_size)]
        down_to = ref.at[pl.ds(slot(n - k) * stride + down_start, down_size)]
        return [
            send(up_from, up_to, send_sem.at[0, k - 1], recv_sem.at[0, k - 1], after),
            send(down_from, down_to, send_sem.at[1, k - 1], recv_sem.at[1, k - 1], before),
        ]

    def across(a, b):
        return lax.dot_general(
            a, b, (((1,), (1,)), ((), ())), precision=lax.Precision.HIGHEST, preferred_element_type=jnp.float32
        )

    def exact(a, b):
        return jnp.dot(a, b, precision=lax.Precision.HIGHEST, preferred_element_type=jnp.float32)

    length, channels = x_ref.shape
    own_heads = dt_ref.shape[0]
    groups = b_ref.shape[1] // STATE
    span = channels // groups
    f32 = jnp.float32
    pending = []

    at_row = lax.broadcasted_iota(jnp.int32, (length, length), 0)
    at_column = lax.broadcasted_iota(jnp.int32, (length, length), 1)
    lower = jnp.where(at_row >= at_column, 1.0, 0.0)
    identity = jnp.where(at_row == at_column, 1.0, 0.0)
    dt_heads = dt_ref[...]
    slow = jnp.concatenate([-rates_ref[...] * dt_heads, jnp.zeros((LANES - own_heads, length), f32)], axis=0)
    logs = across(lower, slow)
    logs_heads = across(slow, lower)
    docs_col, docs_row = docs_col_ref[...], docs_row_ref[...]
    first, last = docs_row[:, :1], docs_row[:, length - 1 :]
    lane = lax.broadcasted_iota(jnp.int32, (1, LANES), 1)
    note = jnp.where(lane == own_heads, first, jnp.where(lane == own_heads + 1, last, logs[length - 1 :]))
    meta_ref[me] = jnp.broadcast_to(note, (8, LANES))
    pl.semaphore_wait(barrier, n)
    notes = [
        send(meta_ref.at[me], meta_ref.at[me], meta_send.at[d], meta_recv.at[d], {"ctx": (me + d) % n})
        for d in range(1, n)
    ]
    pending += notes

    head_row = lax.broadcasted_iota(jnp.int32, (LANES, channels), 0)
    channel = lax.broadcasted_iota(jnp.int32, (LANES, channels), 1)
    spread = jnp.where((channel >= head_row * HEAD_DIM) & (channel < (head_row + 1) * HEAD_DIM), 1.0, 0.0)
    tail = jnp.exp(logs_heads[:own_heads, length - 1 :] - logs_heads[:own_heads])
    tail = tail * jnp.where(docs_row == last, 1.0, 0.0) * dt_heads
    tail = jnp.concatenate([tail, jnp.zeros((LANES - own_heads, length), f32)], axis=0)
    tail = exact(across(identity, tail), spread)
    for g in range(groups):
        part = pl.ds(g * span, span)
        scaled = (x_ref[:, part].astype(f32) * tail[:, g * span : (g + 1) * span]).astype(jnp.bfloat16)
        turned = b_ref[:, pl.ds(g * STATE, STATE)].astype(f32).T.astype(jnp.bfloat16)
        state_ref[pl.ds(0, STATE), part] = jnp.dot(turned, scaled, preferred_element_type=f32).astype(jnp.bfloat16)
    arriving = ring_hop(state_ref, STATE, STATE, state_send, state_recv, 1)
    pending += arriving

    causal = (docs_col == docs_row) & (at_row >= at_column)
    low_lanes = lax.broadcasted_iota(jnp.int32, (length, LANES), 1) < HEAD_DIM
    skip = exact(skip_ref[...], spread)
    for g in range(groups):
        state_part = pl.ds(g * STATE, STATE)
        scores = lax.dot_general(
            c_ref[:, state_part], b_ref[:, state_part], (((1,), (1,)), ((), ())), preferred_element_type=f32
        )
        scores = jnp.where(causal, scores, 0.0)
        for pair in range(g * span // LANES, (g + 1) * span // LANES):
            place_of = pl.ds(pair * LANES, LANES)
            values = x_ref[:, place_of]
            mixes = []
            for h in (2 * pair, 2 * pair + 1):
                gap = jnp.where(causal, logs[:, h : h + 1] - logs_heads[h : h + 1, :], 0.0)
                mixes.append((jnp.exp(gap) * scores * dt_heads[h : h + 1, :]).astype(jnp.bfloat16))
            none = jnp.zeros_like(values)
            sides = jnp.concatenate([jnp.where(low_lanes, values, none), jnp.where(low_lanes, none, values)], axis=0)
            inside = jnp.dot(jnp.concatenate(mixes, axis=1), sides, preferred_element_type=f32)
            scan_ref[:, place_of] = inside + skip[:1, pair * LANES : (pair + 1) * LANES] * values.astype(f32)

    for copy in notes:
        copy.wait_recv()
    running = jnp.zeros((1, LANES), f32)
    kept = [None] * n
    for j in reversed(range(n)):
        line = meta_ref[j][:1]
        earlier = jnp.where(j < me, 1.0, 0.0)
        same = jnp.where(line[:, own_heads + 1 : own_heads + 2] == first, 1.0, 0.0)
        kept[j] = jnp.exp(running) * same * earlier
        running = running + jnp.where(lane < own_heads, line, 0.0) * earlier
    reach_ref[...] = exact(jnp.concatenate(kept, axis=0), spread)

    def add_state(s):
        share_of = reach_ref[pl.ds(ring_index((place + n - s) % n, n), 1), :]
        value = state_ref[pl.ds(slot(s) * STATE, STATE)].astype(f32) * share_of
        if s == 1:
            incoming_ref[...] = value
        else:
            incoming_ref[...] += value

    for k in range(1, half + 1):
        for copy in arriving:
            copy.wait_recv()
        if k < half:
            arriving = ring_hop(state_ref, STATE, STATE, state_send, state_recv, k + 1)
            pending += arriving
        for s in [k, n - k] if k < half else [k]:
            add_state(s)

    since = exact(jnp.exp(logs) * jnp.where(docs_col == docs_col[:1], 1.0, 0.0), spread)
    for g in range(groups):
        part = pl.ds(g * span, span)
        outer = jnp.dot(
            c_ref[:, pl.ds(g * STATE, STATE)], incoming_ref[:, part].astype(jnp.bfloat16), preferred_element_type=f32
        )
        gated = scan_ref[:, part] + outer * since[:, g * span : (g + 1) * span]
        gate_value = silu_ref[:, part].astype(f32)
        gated = gated * silu(gate_value)
        size = jnp.sqrt(jnp.mean(gated * gated, axis=1, keepdims=True) + EPS)
        normed_ref[pl.ds(0, length), part] = (gated / size * norm_ref[:, part]).astype(jnp.bfloat16)

    arriving = ring_hop(normed_ref, length, length, normed_send, normed_recv, 1)
    pending += arriving
    own_rows = pl.ds(pl.multiple_of(head * rows, 16), rows)
    other_rows = pl.ds(pl.multiple_of((1 - head) * rows, 16), rows)
    products = {}

    def project(near):
        value = lax.dot_general(
            normed_ref[pl.ds(slot(near[0]) * length, len(near) * length)],
            proj_ref[...],
            (((1,), (1,)), ((), ())),
            preferred_element_type=f32,
        )
        for i, s in enumerate(near):
            product_ref[slot(s)] = value[i * length : (i + 1) * length]
            product_lent_ref[slot(s)] = product_ref[slot(s), other_rows].astype(jnp.bfloat16)
            products[s] = send(
                product_lent_ref.at[slot(s)],
                product_got_ref.at[slot(s)],
                product_send.at[s],
                product_recv.at[s],
                sibling,
            )

    blocks = []

    def deliver(s):
        products[s].wait_recv()
        value = product_ref[slot(s), own_rows] + product_got_ref[slot(s)].astype(f32)
        if s == 0:
            columns_ref[me] = value.astype(jnp.bfloat16)
            return
        block_ref[s] = value.astype(jnp.bfloat16)
        owner = {"ctx": ring_index((place + n - s) % n, n)}
        blocks.append(send(block_ref.at[s], columns_ref.at[me], block_send.at[s], block_recv.at[s], owner))

    project([0])
    ready = [0]
    for k in range(1, half + 1):
        for copy in arriving:
            copy.wait_recv()
        if k < half:
            arriving = ring_hop(normed_ref, length, length, normed_send, normed_recv, k + 1)
            pending += arriving
        near = [k, n - k] if k < half else [k]
        project(near)
        for s in ready:
            deliver(s)
        ready = near
    for s in ready:
        deliver(s)
    for copy in blocks:
        copy.wait_recv()
    pending += list(products.values()) + blocks
    share_width = proj_ref.shape[0]
    for j in range(n):
        mamba_ref[:, pl.ds(j * share_width, share_width)] = columns_ref[j].astype(f32)

    hidden_ref[...] = (residual_ref[...].astype(f32) + mamba_ref[...]).astype(jnp.bfloat16)
    hidden = hidden_ref[...].astype(f32)
    scale = jnp.sqrt(jnp.mean(hidden * hidden, axis=1, keepdims=True) + EPS)
    rows_ref[pl.ds(0, rows), pl.ds(0, width)] = (hidden / scale * gain_ref[...]).astype(jnp.bfloat16)
    gate = gate_ref[...]
    high = gate.astype(jnp.bfloat16).astype(f32)
    rows_ref[pl.ds(0, rows), pl.ds(width, LANES)] = jnp.where(lane < LANES // 2, high, gate - high).astype(jnp.bfloat16)

    def hop(k):
        return ring_hop(rows_ref, both, rows, ag_send, ag_recv, k)

    def share(s):
        return send(
            rows_ref.at[pl.ds(slot(s) * both, rows)],
            rows_ref.at[pl.ds(slot(s) * both + rows, rows)],
            sib_send.at[slot(s)],
            sib_recv.at[slot(s)],
            sibling,
        )

    column = lax.broadcasted_iota(jnp.int32, (both, LANES), 1)

    def expert(slots):
        count = len(slots) * both
        first = slots[0]
        block = pl.ds(first * both, count)

        def up(columns):
            value = lax.dot_general(
                rows_ref[block, pl.ds(0, width)],
                up_ref[columns, :],
                (((1,), (1,)), ((), ())),
                preferred_element_type=jnp.float32,
            )
            value = jnp.maximum(value, 0.0)
            act_ref[pl.ds(0, count), columns] = (value * value).astype(jnp.bfloat16)

        tile = 2 * LANES

        @pl.loop(0, inner // tile)
        def _(i):
            up(pl.ds(pl.multiple_of(i * tile, tile), tile))

        if inner % tile:
            up(pl.ds(inner // tile * tile, inner % tile))

        weights = []
        for s in slots:
            carried = rows_ref[pl.ds(s * both, both), pl.ds(width, LANES)].astype(jnp.float32)
            chosen = (column == mine) | (column == mine + LANES // 2)
            weights.append(jnp.sum(jnp.where(chosen, carried, 0.0), axis=1, keepdims=True))

        def down(columns):
            value = jnp.dot(
                act_ref[pl.ds(0, count), :], down_ref[:, columns], preferred_element_type=jnp.float32
            )
            for i, s in enumerate(slots):
                own = value[i * both : i * both + rows] * weights[i][:rows]
                other = value[i * both + rows : (i + 1) * both] * weights[i][rows:]
                part_ref[s, :, columns] = own.astype(jnp.bfloat16)
                lent_ref[s, :, columns] = other.astype(jnp.bfloat16)

        wide = width // LANES
        step = max(d for d in (1, 2, 3, 4) if wide % d == 0) * LANES

        @pl.loop(0, width // step)
        def _(i):
            down(pl.ds(pl.multiple_of(i * step, LANES), step))

        return [
            send(lent_ref.at[s], borrowed_ref.at[s], lend_send.at[s], lend_recv.at[s], sibling) for s in slots
        ]

    loans = {}
    started = list(hop(1))
    arriving = started
    shares = {0: share(0)}
    up_copy.wait()
    down_copy.wait()
    shares[0].wait_recv()
    loans[slot(0)] = expert([slot(0)])[0]
    for k in range(1, half + 1):
        for copy in arriving:
            copy.wait_recv()
        if k < half:
            arriving = hop(k + 1)
            started += list(arriving)
        near = [k, n - k] if k < half else [k]
        for s in near:
            shares[s] = share(s)
        for s in near:
            shares[s].wait_recv()
        lent = expert([slot(s) for s in near])
        for s, copy in zip(near, lent):
            loans[slot(s)] = copy

    def total(s, inbound):
        loans[slot(s)].wait_recv()
        value = part_ref[slot(s)].astype(jnp.float32) + borrowed_ref[slot(s)].astype(jnp.float32)
        return value

    backs = []

    def give(s, low, high, down, k):
        piece = pl.ds(low, high - low)
        if down:
            nearer = s - 1 if s > 1 else 0
            return send(
                part_ref.at[slot(s), piece],
                sums_ref.at[slot(nearer), piece],
                rs_send.at[0, k - 1],
                rs_recv.at[0, k - 1],
                before,
            )
        nearer = s + 1 if s + 1 < n else half
        return send(
            part_ref.at[slot(s), piece],
            sums_ref.at[slot(nearer), piece],
            rs_send.at[1, k - 1],
            rs_recv.at[1, k - 1],
            after,
        )

    part_ref[slot(half)] = total(half, None).astype(jnp.bfloat16)
    coming = [give(half, 0, cut, True, half), give(half, cut, rows, False, half)]
    backs += coming
    for k in range(half - 1, 0, -1):
        lower = total(k, None)
        upper = total(n - k, None)
        part_ref[slot(k)] = lower.astype(jnp.bfloat16)
        part_ref[slot(n - k)] = upper.astype(jnp.bfloat16)
        following = []
        for way, (s, copy) in enumerate(zip((k, n - k), coming)):
            copy.wait_recv()
            piece = pl.ds(0, rows)
            if k == half - 1:
                piece = pl.ds(0, cut) if way == 0 else pl.ds(cut, rows - cut)
            value = part_ref[slot(s), piece].astype(jnp.float32) + sums_ref[slot(s), piece].astype(jnp.float32)
            part_ref[slot(s), piece] = value.astype(jnp.bfloat16)
            following.append(give(s, 0, rows, way == 0, k))
        coming = following
        backs += coming
    value = hidden_ref[...].astype(jnp.float32) + total(0, None)
    for copy in coming:
        copy.wait_recv()
    value = value + sums_ref[slot(0)].astype(jnp.float32) + sums_ref[slot(half)].astype(jnp.float32)
    out_ref[...] = value.astype(jnp.bfloat16)
    for copy in pending + started + list(shares.values()) + list(loans.values()) + backs:
        copy.wait_send()


def layer_on_ring(
    channels,
    gate_channels,
    bmat,
    cmat,
    dt,
    rates,
    skip,
    norm_gain,
    docs,
    w_out,
    residual,
    moe_gain,
    experts,
    gates,
    w_up,
    w_down,
):
    n, heads = lax.axis_size("ctx"), lax.axis_size("head")
    rows, width = residual.shape
    length, wide = channels.shape
    inner = w_up.shape[2]
    share_width = w_out.shape[1]
    lane = jnp.arange(LANES, dtype=jnp.int32) % (LANES // 2)
    gate = jnp.sum(jnp.where(experts[:, :, None] == lane[None, None, :], gates[:, :, None], 0.0), axis=1)
    ids = docs.astype(jnp.float32)
    skip_row = jnp.pad(skip[None, :], ((0, 7), (0, LANES - skip.shape[0])))
    vmem = pl.BlockSpec(memory_space=pltpu.VMEM)
    anywhere = pl.BlockSpec(memory_space=pl.ANY)
    bf16, f32 = jnp.bfloat16, jnp.float32
    pieces = pltpu.VMEM((n, rows, width), bf16)
    shares = pltpu.VMEM((n, rows, share_width), bf16)
    ring_sem = pltpu.SemaphoreType.DMA((2, n // 2))
    each_sem = pltpu.SemaphoreType.DMA((n,))
    return pl.pallas_call(
        functools.partial(layer_kernel, n, heads),
        out_shape=jax.ShapeDtypeStruct((rows, width), bf16),
        in_specs=[vmem] * 14 + [anywhere] * 2,
        out_specs=vmem,
        scratch_shapes=[
            pltpu.VMEM((n, 8, LANES), f32),
            pltpu.VMEM((n, wide), f32),
            pltpu.VMEM((n * STATE, wide), bf16),
            pltpu.VMEM((length, wide), f32),
            pltpu.VMEM((STATE, wide), f32),
            pltpu.VMEM((n * length, wide), bf16),
            pltpu.VMEM((n, length, share_width), f32),
            shares,
            shares,
            shares,
            shares,
            pltpu.VMEM((rows, width), f32),
            pltpu.VMEM((rows, width), bf16),
            pltpu.VMEM((n * 2 * rows, width + LANES), bf16),
            pieces,
            pieces,
            pieces,
            pieces,
            pltpu.VMEM((4 * rows, inner), bf16),
            pltpu.VMEM((inner, width), bf16),
            pltpu.VMEM((inner, width), bf16),
            pltpu.SemaphoreType.DMA((2,)),
            each_sem,
            each_sem,
            ring_sem,
            ring_sem,
            ring_sem,
            ring_sem,
            each_sem,
            each_sem,
            each_sem,
            each_sem,
            ring_sem,
            ring_sem,
            each_sem,
            each_sem,
            each_sem,
            each_sem,
            ring_sem,
            ring_sem,
        ],
        compiler_params=pltpu.CompilerParams(
            collective_id=1, has_side_effects=True, vmem_limit_bytes=58 * 2**20
        ),
        cost_estimate=pl.CostEstimate(
            flops=8 * n * rows * width * inner, bytes_accessed=4 * width * inner, transcendentals=0
        ),
    )(
        channels,
        gate_channels,
        bmat,
        cmat,
        dt.T,
        rates[:, None],
        skip_row,
        norm_gain[None, :],
        ids[:, None],
        ids[None, :],
        w_out.T,
        residual,
        moe_gain[None, :],
        gate,
        jnp.swapaxes(w_up, 1, 2),
        w_down,
    )


def ring_fits(n, heads, rows, width):
    return n % 2 == 0 and n >= 4 and heads == 2 and rows % 32 == 0 and width % LANES == 0 and n * heads <= LANES // 2 and 14 * n * rows * width <= 24 * 2**20


def local(
    channels,
    gate_channels,
    bmat,
    cmat,
    dt,
    rates,
    skip,
    norm_gain,
    docs,
    w_out,
    residual,
    moe_gain,
    experts,
    gates,
    w_up,
    w_down,
):
    if ring_fits(lax.axis_size("ctx"), lax.axis_size("head"), *residual.shape):
        return layer_on_ring(
            channels,
            gate_channels,
            bmat,
            cmat,
            dt,
            rates,
            skip,
            norm_gain,
            docs,
            w_out,
            residual,
            moe_gain,
            experts,
            gates,
            w_up,
            w_down,
        )
    length = channels.shape[0]
    heads = dt.shape[1]
    groups = bmat.shape[1] // STATE
    per_group = heads // groups
    logs = jnp.cumsum(-rates[None, :] * dt, axis=0)
    x_wide = channels.astype(jnp.float32).reshape(length, groups, per_group, HEAD_DIM)
    b_split = bmat.reshape(length, groups, STATE)
    c_split = cmat.reshape(length, groups, STATE)
    position = jnp.arange(length, dtype=jnp.int32)
    causal = (docs[:, None] == docs[None, :]) & (position[:, None] >= position[None, :])
    ending = (docs == docs[length - 1]).astype(jnp.float32)
    opening = (docs == docs[0]).astype(jnp.float32)
    stacked = (
        x_wide.transpose(1, 0, 2, 3),
        b_split.transpose(1, 0, 2),
        c_split.transpose(1, 0, 2),
        logs.reshape(length, groups, per_group).transpose(1, 0, 2),
        dt.reshape(length, groups, per_group).transpose(1, 0, 2),
    )
    inner, end_state = lax.map(lambda item: group_terms(item, causal, ending), stacked)
    end_state = end_state.reshape(heads, HEAD_DIM, STATE)
    whole_decay = jnp.exp(logs[length - 1]) * (docs[0] == docs[length - 1]).astype(jnp.float32)
    element = (docs[:1], docs[length - 1 :], whole_decay, end_state)
    identity = (
        jnp.full((1,), -1, jnp.int32),
        jnp.full((1,), -1, jnp.int32),
        jnp.ones((heads,), jnp.float32),
        jnp.zeros_like(end_state),
    )
    _, prior_last, _, incoming = entering(element, "ctx", combine_states, identity)
    linked = (prior_last == docs[:1]).astype(jnp.float32)
    reach = jnp.exp(logs) * opening[:, None] * linked
    outer = jnp.einsum(
        "tgn,ghpn->tghp",
        c_split.astype(jnp.float32),
        incoming.reshape(groups, per_group, HEAD_DIM, STATE),
        precision=lax.Precision.HIGHEST,
    )
    outer = outer * reach.reshape(length, groups, per_group)[:, :, :, None]
    inner = inner.transpose(1, 0, 2, 3)
    scan = (inner + outer).reshape(length, heads, HEAD_DIM) + skip[None, :, None] * x_wide.reshape(
        length, heads, HEAD_DIM
    )
    scan = scan.reshape(length, heads * HEAD_DIM)
    gated = scan * silu(gate_channels.astype(jnp.float32))
    grouped = gated.reshape(length, -1, HEADS * HEAD_DIM // GROUPS)
    grouped = grouped / jnp.sqrt(jnp.mean(grouped * grouped, axis=2, keepdims=True) + EPS)
    normed_scan = (grouped.reshape(length, -1) * norm_gain).astype(jnp.bfloat16)
    partial_value = jnp.dot(
        normed_scan,
        lax.all_gather(w_out, "ctx", axis=1, tiled=True),
        preferred_element_type=jnp.float32,
    )
    mamba_out = lax.psum_scatter(
        partial_value.astype(jnp.bfloat16), "head", scatter_dimension=0, tiled=True
    ).astype(jnp.float32)
    hidden = (residual.astype(jnp.float32) + mamba_out).astype(jnp.bfloat16)
    widened = hidden.astype(jnp.float32)
    moe_in = (
        widened / jnp.sqrt(jnp.mean(widened * widened, axis=1, keepdims=True) + EPS) * moe_gain
    ).astype(jnp.bfloat16)
    rows_dev = moe_in.shape[0]
    top = experts.shape[1]
    width = moe_in.shape[1]
    ctx_count = lax.axis_size("ctx")
    head_count = lax.axis_size("head")
    experts_all = ctx_count * head_count
    capacity = min(rows_dev, max(4, 3 * rows_dev * top // (2 * experts_all)))
    picks = experts.reshape(-1)
    pick_index = jnp.arange(picks.shape[0], dtype=jnp.int32)
    earlier = (picks[:, None] == picks[None, :]) & (pick_index[None, :] < pick_index[:, None])
    slot = jnp.sum(earlier.astype(jnp.int32), axis=1)
    target = (picks * capacity + slot).reshape(rows_dev, top)
    places = jnp.arange(experts_all * capacity, dtype=jnp.int32)
    routing = jnp.any(target[None, :, :] == places[:, None, None], axis=2).astype(jnp.bfloat16)
    outgoing = jnp.dot(routing, moe_in, preferred_element_type=jnp.float32).astype(jnp.bfloat16)
    outgoing = outgoing.reshape(experts_all, capacity, width)
    up_weight = w_up[0]
    down_weight = w_down[0]
    results = expert_rows(
        lax.all_to_all(outgoing, ("ctx", "head"), split_axis=0, concat_axis=0, tiled=True),
        up_weight,
        down_weight,
    )
    returned = lax.all_to_all(results, ("ctx", "head"), split_axis=0, concat_axis=0, tiled=True)
    flat_back = returned.reshape(experts_all * capacity, width)
    chosen = flat_back[target].astype(jnp.float32)
    mixture = jnp.sum(chosen * gates[:, :, None], axis=1)
    return (widened + mixture).astype(jnp.bfloat16)


def solution(mesh):
    return jax.shard_map(
        local,
        mesh=mesh,
        in_specs=(
            P(("parts", "ctx"), "head"),
            P(("parts", "ctx"), "head"),
            P(("parts", "ctx"), "head"),
            P(("parts", "ctx"), "head"),
            P(("parts", "ctx"), "head"),
            P("head"),
            P("head"),
            P("head"),
            P(("parts", "ctx")),
            P("head", "ctx"),
            P(("parts", "ctx", "head"), None),
            P(),
            P(("parts", "ctx", "head"), None),
            P(("parts", "ctx", "head"), None),
            P(("ctx", "head"), None, None),
            P(("ctx", "head"), None, None),
        ),
        out_specs=P(("parts", "ctx", "head"), None),
        check_vma=False,
    )
```

```python
import functools

import jax
import jax.numpy as jnp
from jax import lax
from jax.experimental import pallas as pl
from jax.experimental.pallas import tpu as pltpu
from jax.sharding import PartitionSpec as P

HEADS = 32
HEAD_DIM = 64
GROUPS = 4
STATE = 128


EPS = 1e-05


def entering(array, axis, combine, identity):
    size, place = (lax.axis_size(axis), lax.axis_index(axis))
    everything = jax.tree.map(lambda part: lax.all_gather(part, axis), array)
    start = jax.tree.map(
        lambda part, zero: jnp.broadcast_to(jnp.asarray(zero, part.dtype), part.shape),
        array,
        identity,
    )

    def lap(k, before):
        reached = k < place
        new = combine(before, jax.tree.map(lambda part: part[k], everything))
        return jax.tree.map(lambda a, b: jnp.where(reached, a, b), new, before)

    return lax.fori_loop(0, size, lap, start)


def silu(value):
    return value / (1.0 + jnp.exp(-value))


def combine_states(earlier, later):
    first_a, last_a, decay_a, state_a = earlier
    first_b, last_b, decay_b, state_b = later
    linked = ((last_a == first_b) | (last_a < 0) | (first_b < 0)).astype(jnp.float32)
    carried = decay_b * linked
    decay = carried * decay_a
    state = state_b + carried[:, None, None] * state_a
    first = jnp.where(first_a < 0, first_b, first_a)
    last = jnp.where(last_b < 0, last_a, last_b)
    return (first, last, decay, state)


def group_terms(inputs, causal, ending):
    x_group, b_group, c_group, log_group, dt_group = inputs
    scores = jnp.dot(c_group, b_group.T, preferred_element_type=jnp.float32)
    gap = jnp.where(causal[:, :, None], log_group[:, None, :] - log_group[None, :, :], -jnp.inf)
    weight = jnp.exp(gap) * scores[:, :, None] * dt_group[None, :, :]
    inner = jnp.einsum("tsh,shp->thp", weight, x_group, precision=lax.Precision.HIGHEST)
    tail = jnp.exp(log_group[-1][None, :] - log_group) * ending[:, None] * dt_group
    end_state = jnp.einsum(
        "sh,shp,sn->hpn",
        tail,
        x_group,
        b_group.astype(jnp.float32),
        precision=lax.Precision.HIGHEST,
    )
    return (inner, end_state)


def expert_rows(received, up_weight, down_weight):
    sources, items, width = received.shape
    rows = received.reshape(sources * items, width)
    up = jnp.dot(rows, up_weight, preferred_element_type=jnp.float32)
    act = jnp.square(jnp.maximum(up, 0.0)).astype(jnp.bfloat16)
    result = jnp.dot(act, down_weight, preferred_element_type=jnp.float32).astype(jnp.bfloat16)
    return result.reshape(sources, items, width)


MESH = pl.DeviceIdType.MESH
LANES = 128


def ring_place(index, size):
    half, odd = index // 2, index % 2
    return (1 - odd) * half + odd * (size - 1 - half)


def ring_index(place, size):
    back = place // (size // 2)
    return (1 - back) * (2 * place) + back * (2 * (size - 1 - place) + 1)


def layer_kernel(
    n,
    heads,
    x_ref,
    silu_ref,
    b_ref,
    c_ref,
    dt_ref,
    rates_ref,
    skip_ref,
    norm_ref,
    docs_row_ref,
    proj_ref,
    residual_ref,
    gain_ref,
    gate_ref,
    up_hbm,
    down_hbm,
    out_ref,
    meta_ref,
    reach_ref,
    state_ref,
    scan_ref,
    incoming_ref,
    normed_ref,
    product_ref,
    product_lent_ref,
    product_got_ref,
    block_ref,
    columns_ref,
    mamba_ref,
    hidden_ref,
    rows_ref,
    part_ref,
    lent_ref,
    borrowed_ref,
    sums_ref,
    act_ref,
    up_ref,
    down_ref,
    weight_sem,
    meta_send,
    meta_recv,
    state_send,
    state_recv,
    normed_send,
    normed_recv,
    product_send,
    product_recv,
    block_send,
    block_recv,
    ag_send,
    ag_recv,
    sib_send,
    sib_recv,
    lend_send,
    lend_recv,
    rs_send,
    rs_recv,
):
    rows, width = residual_ref.shape
    both = 2 * rows
    inner = up_ref.shape[0]
    half = n // 2
    cut = rows // 2
    place = ring_place(lax.axis_index("ctx"), n)
    head = lax.axis_index("head")
    mine = lax.axis_index("ctx") * heads + head
    after = {"ctx": ring_index((place + 1) % n, n)}
    before = {"ctx": ring_index((place + n - 1) % n, n)}
    sibling = {"head": 1 - head}

    up_copy = pltpu.make_async_copy(up_hbm.at[0], up_ref, weight_sem.at[0])
    down_copy = pltpu.make_async_copy(down_hbm.at[0], down_ref, weight_sem.at[1])
    up_copy.start()
    down_copy.start()

    me = lax.axis_index("ctx")
    barrier = pltpu.get_barrier_semaphore()
    for d in range(1, n):
        pl.semaphore_signal(barrier, inc=1, device_id={"ctx": (me + d) % n}, device_id_type=MESH)
    pl.semaphore_signal(barrier, inc=1, device_id=sibling, device_id_type=MESH)

    def slot(s):
        if s == 0:
            return 0
        if s == half:
            return 1
        return 2 * s if s < half else 2 * (n - s) + 1

    def send(source, target, send_sem, recv_sem, device):
        copy = pltpu.make_async_remote_copy(
            src_ref=source,
            dst_ref=target,
            send_sem=send_sem,
            recv_sem=recv_sem,
            device_id=device,
            device_id_type=MESH,
        )
        copy.start()
        return copy

    def ring_hop(ref, stride, size, send_sem, recv_sem, k):
        up_start, up_size, down_start, down_size = 0, size, 0, size
        if k == half:
            up_size, down_start, down_size = size // 2, size // 2, size // 2
        up_from = ref.at[pl.ds(slot(k - 1) * stride + up_start, up_size)]
        up_to = ref.at[pl.ds(slot(k) * stride + up_start, up_size)]
        down_from = ref.at[pl.ds(slot((n - k + 1) % n) * stride + down_start, down_size)]
        down_to = ref.at[pl.ds(slot(n - k) * stride + down_start, down_size)]
        return [
            send(up_from, up_to, send_sem.at[0, k - 1], recv_sem.at[0, k - 1], after),
            send(down_from, down_to, send_sem.at[1, k - 1], recv_sem.at[1, k - 1], before),
        ]

    def across(a, b):
        return lax.dot_general(
            a, b, (((1,), (1,)), ((), ())), precision=lax.Precision.HIGHEST, preferred_element_type=jnp.float32
        )

    def exact(a, b):
        return jnp.dot(a, b, precision=lax.Precision.HIGHEST, preferred_element_type=jnp.float32)

    length, channels = x_ref.shape
    own_heads = dt_ref.shape[0]
    groups = b_ref.shape[1] // STATE
    span = channels // groups
    f32 = jnp.float32
    pending = []

    at_row = lax.broadcasted_iota(jnp.int32, (length, length), 0)
    at_column = lax.broadcasted_iota(jnp.int32, (length, length), 1)
    lower = jnp.where(at_row >= at_column, 1.0, 0.0)
    identity = jnp.where(at_row == at_column, 1.0, 0.0)
    dt_heads = dt_ref[...]
    rates = across(identity[:own_heads, :own_heads], jnp.broadcast_to(rates_ref[...], (8, own_heads)))[:, :1]
    slow = jnp.concatenate([-rates * dt_heads, jnp.zeros((LANES - own_heads, length), f32)], axis=0)
    logs = across(lower, slow)
    logs_heads = across(slow, lower)
    docs_row = docs_row_ref[...].astype(f32)
    docs_col = across(identity, jnp.broadcast_to(docs_row, (8, length)))[:, :1]
    first, last = docs_row[:, :1], docs_row[:, length - 1 :]
    lane = lax.broadcasted_iota(jnp.int32, (1, LANES), 1)
    note = jnp.where(lane == own_heads, first, jnp.where(lane == own_heads + 1, last, logs[length - 1 :]))
    meta_ref[me] = jnp.broadcast_to(note, (8, LANES))
    pl.semaphore_wait(barrier, n)
    notes = [
        send(meta_ref.at[me], meta_ref.at[me], meta_send.at[d], meta_recv.at[d], {"ctx": (me + d) % n})
        for d in range(1, n)
    ]
    pending += notes

    head_row = lax.broadcasted_iota(jnp.int32, (LANES, channels), 0)
    channel = lax.broadcasted_iota(jnp.int32, (LANES, channels), 1)
    spread = jnp.where((channel >= head_row * HEAD_DIM) & (channel < (head_row + 1) * HEAD_DIM), 1.0, 0.0)
    tail = jnp.exp(logs_heads[:own_heads, length - 1 :] - logs_heads[:own_heads])
    tail = tail * jnp.where(docs_row == last, 1.0, 0.0) * dt_heads
    tail = jnp.concatenate([tail, jnp.zeros((LANES - own_heads, length), f32)], axis=0)
    tail = exact(across(identity, tail), spread)
    for g in range(groups):
        part = pl.ds(g * span, span)
        scaled = (x_ref[:, part].astype(f32) * tail[:, g * span : (g + 1) * span]).astype(jnp.bfloat16)
        turned = b_ref[:, pl.ds(g * STATE, STATE)].astype(f32).T.astype(jnp.bfloat16)
        state_ref[pl.ds(0, STATE), part] = jnp.dot(turned, scaled, preferred_element_type=f32).astype(jnp.bfloat16)
    arriving = ring_hop(state_ref, STATE, STATE, state_send, state_recv, 1)
    pending += arriving

    causal = (docs_col == docs_row) & (at_row >= at_column)
    low_lanes = lax.broadcasted_iota(jnp.int32, (length, LANES), 1) < HEAD_DIM
    skip = exact(jnp.broadcast_to(skip_ref[...], (8, own_heads)), spread[:own_heads])
    for g in range(groups):
        state_part = pl.ds(g * STATE, STATE)
        scores = lax.dot_general(
            c_ref[:, state_part], b_ref[:, state_part], (((1,), (1,)), ((), ())), preferred_element_type=f32
        )
        scores = jnp.where(causal, scores, 0.0)
        for pair in range(g * span // LANES, (g + 1) * span // LANES):
            place_of = pl.ds(pair * LANES, LANES)
            values = x_ref[:, place_of]
            mixes = []
            for h in (2 * pair, 2 * pair + 1):
                gap = jnp.where(causal, logs[:, h : h + 1] - logs_heads[h : h + 1, :], 0.0)
                mixes.append((jnp.exp(gap) * scores * dt_heads[h : h + 1, :]).astype(jnp.bfloat16))
            none = jnp.zeros_like(values)
            sides = jnp.concatenate([jnp.where(low_lanes, values, none), jnp.where(low_lanes, none, values)], axis=0)
            inside = jnp.dot(jnp.concatenate(mixes, axis=1), sides, preferred_element_type=f32)
            scan_ref[:, place_of] = inside + skip[:1, pair * LANES : (pair + 1) * LANES] * values.astype(f32)

    for copy in notes:
        copy.wait_recv()
    running = jnp.zeros((1, LANES), f32)
    kept = [None] * n
    for j in reversed(range(n)):
        line = meta_ref[j][:1]
        earlier = jnp.where(j < me, 1.0, 0.0)
        same = jnp.where(line[:, own_heads + 1 : own_heads + 2] == first, 1.0, 0.0)
        kept[j] = jnp.exp(running) * same * earlier
        running = running + jnp.where(lane < own_heads, line, 0.0) * earlier
    reach_ref[...] = exact(jnp.concatenate(kept, axis=0), spread)

    def add_state(s):
        share_of = reach_ref[pl.ds(ring_index((place + n - s) % n, n), 1), :]
        value = state_ref[pl.ds(slot(s) * STATE, STATE)].astype(f32) * share_of
        if s == 1:
            incoming_ref[...] = value
        else:
            incoming_ref[...] += value

    for k in range(1, half + 1):
        for copy in arriving:
            copy.wait_recv()
        if k < half:
            arriving = ring_hop(state_ref, STATE, STATE, state_send, state_recv, k + 1)
            pending += arriving
        for s in [k, n - k] if k < half else [k]:
            add_state(s)

    since = exact(jnp.exp(logs) * jnp.where(docs_col == docs_col[:1], 1.0, 0.0), spread)
    for g in range(groups):
        part = pl.ds(g * span, span)
        outer = jnp.dot(
            c_ref[:, pl.ds(g * STATE, STATE)], incoming_ref[:, part].astype(jnp.bfloat16), preferred_element_type=f32
        )
        gated = scan_ref[:, part] + outer * since[:, g * span : (g + 1) * span]
        gate_value = silu_ref[:, part].astype(f32)
        gated = gated * silu(gate_value)
        size = jnp.sqrt(jnp.mean(gated * gated, axis=1, keepdims=True) + EPS)
        normed_ref[pl.ds(0, length), part] = (gated / size * norm_ref[:, part]).astype(jnp.bfloat16)

    arriving = ring_hop(normed_ref, length, length, normed_send, normed_recv, 1)
    pending += arriving
    own_rows = pl.ds(pl.multiple_of(head * rows, 16), rows)
    other_rows = pl.ds(pl.multiple_of((1 - head) * rows, 16), rows)
    products = {}

    def project(near):
        value = lax.dot_general(
            normed_ref[pl.ds(slot(near[0]) * length, len(near) * length)],
            proj_ref[...],
            (((1,), (1,)), ((), ())),
            preferred_element_type=f32,
        )
        for i, s in enumerate(near):
            product_ref[slot(s)] = value[i * length : (i + 1) * length]
            product_lent_ref[slot(s)] = product_ref[slot(s), other_rows].astype(jnp.bfloat16)
            products[s] = send(
                product_lent_ref.at[slot(s)],
                product_got_ref.at[slot(s)],
                product_send.at[s],
                product_recv.at[s],
                sibling,
            )

    blocks = []

    def deliver(s):
        products[s].wait_recv()
        value = product_ref[slot(s), own_rows] + product_got_ref[slot(s)].astype(f32)
        if s == 0:
            columns_ref[me] = value.astype(jnp.bfloat16)
            return
        block_ref[s] = value.astype(jnp.bfloat16)
        owner = {"ctx": ring_index((place + n - s) % n, n)}
        blocks.append(send(block_ref.at[s], columns_ref.at[me], block_send.at[s], block_recv.at[s], owner))

    project([0])
    ready = [0]
    for k in range(1, half + 1):
        for copy in arriving:
            copy.wait_recv()
        if k < half:
            arriving = ring_hop(normed_ref, length, length, normed_send, normed_recv, k + 1)
            pending += arriving
        near = [k, n - k] if k < half else [k]
        project(near)
        for s in ready:
            deliver(s)
        ready = near
    for s in ready:
        deliver(s)
    for copy in blocks:
        copy.wait_recv()
    pending += list(products.values()) + blocks
    share_width = proj_ref.shape[0]
    for j in range(n):
        mamba_ref[:, pl.ds(j * share_width, share_width)] = columns_ref[j].astype(f32)

    hidden_ref[...] = (residual_ref[...].astype(f32) + mamba_ref[...]).astype(jnp.bfloat16)
    hidden = hidden_ref[...].astype(f32)
    scale = jnp.sqrt(jnp.mean(hidden * hidden, axis=1, keepdims=True) + EPS)
    rows_ref[pl.ds(0, rows), pl.ds(0, width)] = (hidden / scale * gain_ref[...]).astype(jnp.bfloat16)
    gate = gate_ref[...]
    high = gate.astype(jnp.bfloat16).astype(f32)
    rows_ref[pl.ds(0, rows), pl.ds(width, LANES)] = jnp.where(lane < LANES // 2, high, gate - high).astype(jnp.bfloat16)

    def hop(k):
        return ring_hop(rows_ref, both, rows, ag_send, ag_recv, k)

    def share(s):
        return send(
            rows_ref.at[pl.ds(slot(s) * both, rows)],
            rows_ref.at[pl.ds(slot(s) * both + rows, rows)],
            sib_send.at[slot(s)],
            sib_recv.at[slot(s)],
            sibling,
        )

    column = lax.broadcasted_iota(jnp.int32, (both, LANES), 1)

    def expert(slots):
        count = len(slots) * both
        first = slots[0]
        block = pl.ds(first * both, count)

        def up(columns):
            value = lax.dot_general(
                rows_ref[block, pl.ds(0, width)],
                up_ref[columns, :],
                (((1,), (1,)), ((), ())),
                preferred_element_type=jnp.float32,
            )
            value = jnp.maximum(value, 0.0)
            act_ref[pl.ds(0, count), columns] = (value * value).astype(jnp.bfloat16)

        tile = 2 * LANES

        @pl.loop(0, inner // tile)
        def _(i):
            up(pl.ds(pl.multiple_of(i * tile, tile), tile))

        if inner % tile:
            up(pl.ds(inner // tile * tile, inner % tile))

        weights = []
        for s in slots:
            carried = rows_ref[pl.ds(s * both, both), pl.ds(width, LANES)].astype(jnp.float32)
            chosen = (column == mine) | (column == mine + LANES // 2)
            weights.append(jnp.sum(jnp.where(chosen, carried, 0.0), axis=1, keepdims=True))

        def down(columns):
            value = jnp.dot(
                act_ref[pl.ds(0, count), :], down_ref[:, columns], preferred_element_type=jnp.float32
            )
            for i, s in enumerate(slots):
                own = value[i * both : i * both + rows] * weights[i][:rows]
                other = value[i * both + rows : (i + 1) * both] * weights[i][rows:]
                part_ref[s, :, columns] = own.astype(jnp.bfloat16)
                lent_ref[s, :, columns] = other.astype(jnp.bfloat16)

        wide = width // LANES
        step = max(d for d in (1, 2, 3, 4) if wide % d == 0) * LANES

        @pl.loop(0, width // step)
        def _(i):
            down(pl.ds(pl.multiple_of(i * step, LANES), step))

        return [
            send(lent_ref.at[s], borrowed_ref.at[s], lend_send.at[s], lend_recv.at[s], sibling) for s in slots
        ]

    loans = {}
    started = list(hop(1))
    arriving = started
    shares = {0: share(0)}
    up_copy.wait()
    down_copy.wait()
    shares[0].wait_recv()
    loans[slot(0)] = expert([slot(0)])[0]
    for k in range(1, half + 1):
        for copy in arriving:
            copy.wait_recv()
        if k < half:
            arriving = hop(k + 1)
            started += list(arriving)
        near = [k, n - k] if k < half else [k]
        for s in near:
            shares[s] = share(s)
        for s in near:
            shares[s].wait_recv()
        lent = expert([slot(s) for s in near])
        for s, copy in zip(near, lent):
            loans[slot(s)] = copy

    def total(s, inbound):
        loans[slot(s)].wait_recv()
        value = part_ref[slot(s)].astype(jnp.float32) + borrowed_ref[slot(s)].astype(jnp.float32)
        return value

    backs = []

    def give(s, low, high, down, k):
        piece = pl.ds(low, high - low)
        if down:
            nearer = s - 1 if s > 1 else 0
            return send(
                part_ref.at[slot(s), piece],
                sums_ref.at[slot(nearer), piece],
                rs_send.at[0, k - 1],
                rs_recv.at[0, k - 1],
                before,
            )
        nearer = s + 1 if s + 1 < n else half
        return send(
            part_ref.at[slot(s), piece],
            sums_ref.at[slot(nearer), piece],
            rs_send.at[1, k - 1],
            rs_recv.at[1, k - 1],
            after,
        )

    part_ref[slot(half)] = total(half, None).astype(jnp.bfloat16)
    coming = [give(half, 0, cut, True, half), give(half, cut, rows, False, half)]
    backs += coming
    for k in range(half - 1, 0, -1):
        lower = total(k, None)
        upper = total(n - k, None)
        part_ref[slot(k)] = lower.astype(jnp.bfloat16)
        part_ref[slot(n - k)] = upper.astype(jnp.bfloat16)
        following = []
        for way, (s, copy) in enumerate(zip((k, n - k), coming)):
            copy.wait_recv()
            piece = pl.ds(0, rows)
            if k == half - 1:
                piece = pl.ds(0, cut) if way == 0 else pl.ds(cut, rows - cut)
            value = part_ref[slot(s), piece].astype(jnp.float32) + sums_ref[slot(s), piece].astype(jnp.float32)
            part_ref[slot(s), piece] = value.astype(jnp.bfloat16)
            following.append(give(s, 0, rows, way == 0, k))
        coming = following
        backs += coming
    value = hidden_ref[...].astype(jnp.float32) + total(0, None)
    for copy in coming:
        copy.wait_recv()
    value = value + sums_ref[slot(0)].astype(jnp.float32) + sums_ref[slot(half)].astype(jnp.float32)
    out_ref[...] = value.astype(jnp.bfloat16)
    for copy in pending + started + list(shares.values()) + list(loans.values()) + backs:
        copy.wait_send()


def layer_on_ring(
    channels,
    gate_channels,
    bmat,
    cmat,
    dt,
    rates,
    skip,
    norm_gain,
    docs,
    w_out,
    residual,
    moe_gain,
    experts,
    gates,
    w_up,
    w_down,
):
    n, heads = lax.axis_size("ctx"), lax.axis_size("head")
    rows, width = residual.shape
    length, wide = channels.shape
    inner = w_up.shape[2]
    share_width = w_out.shape[1]
    lane = jnp.arange(LANES, dtype=jnp.int32) % (LANES // 2)
    gate = jnp.sum(jnp.where(experts[:, :, None] == lane[None, None, :], gates[:, :, None], 0.0), axis=1)
    vmem = pl.BlockSpec(memory_space=pltpu.VMEM)
    anywhere = pl.BlockSpec(memory_space=pl.ANY)
    bf16, f32 = jnp.bfloat16, jnp.float32
    pieces = pltpu.VMEM((n, rows, width), bf16)
    shares = pltpu.VMEM((n, rows, share_width), bf16)
    ring_sem = pltpu.SemaphoreType.DMA((2, n // 2))
    each_sem = pltpu.SemaphoreType.DMA((n,))
    return pl.pallas_call(
        functools.partial(layer_kernel, n, heads),
        out_shape=jax.ShapeDtypeStruct((rows, width), bf16),
        in_specs=[vmem] * 13 + [anywhere] * 2,
        out_specs=vmem,
        scratch_shapes=[
            pltpu.VMEM((n, 8, LANES), f32),
            pltpu.VMEM((n, wide), f32),
            pltpu.VMEM((n * STATE, wide), bf16),
            pltpu.VMEM((length, wide), f32),
            pltpu.VMEM((STATE, wide), f32),
            pltpu.VMEM((n * length, wide), bf16),
            pltpu.VMEM((n, length, share_width), f32),
            shares,
            shares,
            shares,
            shares,
            pltpu.VMEM((rows, width), f32),
            pltpu.VMEM((rows, width), bf16),
            pltpu.VMEM((n * 2 * rows, width + LANES), bf16),
            pieces,
            pieces,
            pieces,
            pieces,
            pltpu.VMEM((4 * rows, inner), bf16),
            pltpu.VMEM((inner, width), bf16),
            pltpu.VMEM((inner, width), bf16),
            pltpu.SemaphoreType.DMA((2,)),
            each_sem,
            each_sem,
            ring_sem,
            ring_sem,
            ring_sem,
            ring_sem,
            each_sem,
            each_sem,
            each_sem,
            each_sem,
            ring_sem,
            ring_sem,
            each_sem,
            each_sem,
            each_sem,
            each_sem,
            ring_sem,
            ring_sem,
        ],
        compiler_params=pltpu.CompilerParams(
            collective_id=1, has_side_effects=True, vmem_limit_bytes=58 * 2**20
        ),
        cost_estimate=pl.CostEstimate(
            flops=8 * n * rows * width * inner, bytes_accessed=4 * width * inner, transcendentals=0
        ),
    )(
        channels,
        gate_channels,
        bmat,
        cmat,
        dt.T,
        rates[None, :],
        skip[None, :],
        norm_gain[None, :],
        docs[None, :],
        w_out.T,
        residual,
        moe_gain[None, :],
        gate,
        jnp.swapaxes(w_up, 1, 2),
        w_down,
    )


def ring_fits(n, heads, rows, width):
    return n % 2 == 0 and n >= 4 and heads == 2 and rows % 32 == 0 and width % LANES == 0 and n * heads <= LANES // 2 and 14 * n * rows * width <= 24 * 2**20


def local(
    channels,
    gate_channels,
    bmat,
    cmat,
    dt,
    rates,
    skip,
    norm_gain,
    docs,
    w_out,
    residual,
    moe_gain,
    experts,
    gates,
    w_up,
    w_down,
):
    if ring_fits(lax.axis_size("ctx"), lax.axis_size("head"), *residual.shape):
        return layer_on_ring(
            channels,
            gate_channels,
            bmat,
            cmat,
            dt,
            rates,
            skip,
            norm_gain,
            docs,
            w_out,
            residual,
            moe_gain,
            experts,
            gates,
            w_up,
            w_down,
        )
    length = channels.shape[0]
    heads = dt.shape[1]
    groups = bmat.shape[1] // STATE
    per_group = heads // groups
    logs = jnp.cumsum(-rates[None, :] * dt, axis=0)
    x_wide = channels.astype(jnp.float32).reshape(length, groups, per_group, HEAD_DIM)
    b_split = bmat.reshape(length, groups, STATE)
    c_split = cmat.reshape(length, groups, STATE)
    position = jnp.arange(length, dtype=jnp.int32)
    causal = (docs[:, None] == docs[None, :]) & (position[:, None] >= position[None, :])
    ending = (docs == docs[length - 1]).astype(jnp.float32)
    opening = (docs == docs[0]).astype(jnp.float32)
    stacked = (
        x_wide.transpose(1, 0, 2, 3),
        b_split.transpose(1, 0, 2),
        c_split.transpose(1, 0, 2),
        logs.reshape(length, groups, per_group).transpose(1, 0, 2),
        dt.reshape(length, groups, per_group).transpose(1, 0, 2),
    )
    inner, end_state = lax.map(lambda item: group_terms(item, causal, ending), stacked)
    end_state = end_state.reshape(heads, HEAD_DIM, STATE)
    whole_decay = jnp.exp(logs[length - 1]) * (docs[0] == docs[length - 1]).astype(jnp.float32)
    element = (docs[:1], docs[length - 1 :], whole_decay, end_state)
    identity = (
        jnp.full((1,), -1, jnp.int32),
        jnp.full((1,), -1, jnp.int32),
        jnp.ones((heads,), jnp.float32),
        jnp.zeros_like(end_state),
    )
    _, prior_last, _, incoming = entering(element, "ctx", combine_states, identity)
    linked = (prior_last == docs[:1]).astype(jnp.float32)
    reach = jnp.exp(logs) * opening[:, None] * linked
    outer = jnp.einsum(
        "tgn,ghpn->tghp",
        c_split.astype(jnp.float32),
        incoming.reshape(groups, per_group, HEAD_DIM, STATE),
        precision=lax.Precision.HIGHEST,
    )
    outer = outer * reach.reshape(length, groups, per_group)[:, :, :, None]
    inner = inner.transpose(1, 0, 2, 3)
    scan = (inner + outer).reshape(length, heads, HEAD_DIM) + skip[None, :, None] * x_wide.reshape(
        length, heads, HEAD_DIM
    )
    scan = scan.reshape(length, heads * HEAD_DIM)
    gated = scan * silu(gate_channels.astype(jnp.float32))
    grouped = gated.reshape(length, -1, HEADS * HEAD_DIM // GROUPS)
    grouped = grouped / jnp.sqrt(jnp.mean(grouped * grouped, axis=2, keepdims=True) + EPS)
    normed_scan = (grouped.reshape(length, -1) * norm_gain).astype(jnp.bfloat16)
    partial_value = jnp.dot(
        normed_scan,
        lax.all_gather(w_out, "ctx", axis=1, tiled=True),
        preferred_element_type=jnp.float32,
    )
    mamba_out = lax.psum_scatter(
        partial_value.astype(jnp.bfloat16), "head", scatter_dimension=0, tiled=True
    ).astype(jnp.float32)
    hidden = (residual.astype(jnp.float32) + mamba_out).astype(jnp.bfloat16)
    widened = hidden.astype(jnp.float32)
    moe_in = (
        widened / jnp.sqrt(jnp.mean(widened * widened, axis=1, keepdims=True) + EPS) * moe_gain
    ).astype(jnp.bfloat16)
    rows_dev = moe_in.shape[0]
    top = experts.shape[1]
    width = moe_in.shape[1]
    ctx_count = lax.axis_size("ctx")
    head_count = lax.axis_size("head")
    experts_all = ctx_count * head_count
    capacity = min(rows_dev, max(4, 3 * rows_dev * top // (2 * experts_all)))
    picks = experts.reshape(-1)
    pick_index = jnp.arange(picks.shape[0], dtype=jnp.int32)
    earlier = (picks[:, None] == picks[None, :]) & (pick_index[None, :] < pick_index[:, None])
    slot = jnp.sum(earlier.astype(jnp.int32), axis=1)
    target = (picks * capacity + slot).reshape(rows_dev, top)
    places = jnp.arange(experts_all * capacity, dtype=jnp.int32)
    routing = jnp.any(target[None, :, :] == places[:, None, None], axis=2).astype(jnp.bfloat16)
    outgoing = jnp.dot(routing, moe_in, preferred_element_type=jnp.float32).astype(jnp.bfloat16)
    outgoing = outgoing.reshape(experts_all, capacity, width)
    up_weight = w_up[0]
    down_weight = w_down[0]
    results = expert_rows(
        lax.all_to_all(outgoing, ("ctx", "head"), split_axis=0, concat_axis=0, tiled=True),
        up_weight,
        down_weight,
    )
    returned = lax.all_to_all(results, ("ctx", "head"), split_axis=0, concat_axis=0, tiled=True)
    flat_back = returned.reshape(experts_all * capacity, width)
    chosen = flat_back[target].astype(jnp.float32)
    mixture = jnp.sum(chosen * gates[:, :, None], axis=1)
    return (widened + mixture).astype(jnp.bfloat16)


def solution(mesh):
    return jax.shard_map(
        local,
        mesh=mesh,
        in_specs=(
            P(("parts", "ctx"), "head"),
            P(("parts", "ctx"), "head"),
            P(("parts", "ctx"), "head"),
            P(("parts", "ctx"), "head"),
            P(("parts", "ctx"), "head"),
            P("head"),
            P("head"),
            P("head"),
            P(("parts", "ctx")),
            P("head", "ctx"),
            P(("parts", "ctx", "head"), None),
            P(),
            P(("parts", "ctx", "head"), None),
            P(("parts", "ctx", "head"), None),
            P(("ctx", "head"), None, None),
            P(("ctx", "head"), None, None),
        ),
        out_specs=P(("parts", "ctx", "head"), None),
        check_vma=False,
    )
```
